32 devices in a mesh: row: 8 (over z, x), col: 4 (over y, core).
Axes of the slice: x: 2, y: 2, z: 4, core: 2. Of those that a mesh axis runs over, the one named last changes fastest.
Arguments:
- src_points: bfloat16 [128, 64, 1024], P('row', 'col'), may hold values from -1.5 to 1.5
- dst_points: bfloat16 [16, 64, 1024], P('col', 'row'), may hold values from -1.5 to 1.5
- support: int32 [128, 8], P('row'), may hold values from 0 to 15, as said below
- log_src_mass: float32 [128, 1024], P('row'), may hold values from -1 to 1
- log_dst_mass: float32 [16, 1024], P('col'), may hold values from -1 to 1
- dst_potential: float32 [16, 1024], P('col'), may hold values from -4 to 114
Outputs:
- src_potential_new: float32 [128, 1024], P('row')
- dst_potential_new: float32 [16, 1024], P('col')
The draws below stay inside these ranges and needn't reach their ends.
Inputs may be any that keep to these rules, and one draw needn't show every extreme that they name: `support`: each row cluster names 8 different column clusters; column cluster b belongs to col index b // 4; the col indices that one row cluster names lie in 3 cyclically consecutive indices of col, each of them named at least once; every column cluster is named by some row cluster; for every index of row and every index of col, at most 12 of the 16 row clusters of that row index name a column cluster of that col index, and some pair reaches 12.
All inputs are finite; a program needn't handle non-finite values.
Results may differ from the reference program's by a relative error of at most 0.0003.
Values may be sent and summed in bfloat16 or wider, within the bound.
A program may use at most 64 MiB of HBM per device.

```python
import jax
import jax.numpy as jnp
from jax import lax

DIM = 64
PTS = 1024
K = 8
CCD = 4
RC = 128
CC = 16
N_COL = 4


def draw_support(key, part):
    window = min((K + CCD - 1) // CCD + 1, N_COL)
    places = window * CCD
    keys = jax.random.split(jax.random.fold_in(key, 17), 2)
    clusters = jnp.arange(RC, dtype=jnp.int32)
    first_dev = clusters % N_COL
    forced = clusters // N_COL % CCD
    slots = jnp.arange(places, dtype=jnp.int32)
    slot_dev = slots // CCD
    slot_col = slots % CCD
    picks = jax.random.randint(keys[0], (RC, window), 0, CCD).astype(jnp.int32)
    picks = jnp.where(jnp.arange(window, dtype=jnp.int32)[None, :] == 0, forced[:, None], picks)
    mandatory = (slot_col[None, :] == picks[:, slot_dev]).astype(jnp.int32)
    device = (first_dev[:, None] + slot_dev[None, :]) % N_COL
    hot = (device < max(N_COL // 4, 1)).astype(jnp.int32)
    noise = jax.random.randint(keys[1], (RC, places), 0, 1024).astype(jnp.int32)
    score = (mandatory * 100000 + noise + hot * 600 + (window - slot_dev[None, :]) * 100) * places + slots[None, :]
    unused, idx = lax.top_k(score, K)
    chosen_dev = jnp.take_along_axis(device, idx, axis=1)
    return (chosen_dev * CCD + idx % CCD).astype(jnp.int32)


def draw_dst_potential(key, part):
    keys = jax.random.split(key, 1)
    shape = (CC, PTS)
    return jax.random.truncated_normal(keys[0], -4.0, 4.0, shape, jnp.float32)


def steps_of(stream_key, shape, cuts, smallest, top_value):
    factor_of = 1.0
    for axis_at, shards_of in cuts:
        steps = jax.random.uniform(jax.random.fold_in(jax.random.fold_in(stream_key, 6), axis_at), (shards_of,), jnp.float32, smallest / len(cuts), top_value / len(cuts))
        factor_of = factor_of * jnp.repeat(jnp.exp(steps), shape[axis_at] // shards_of).reshape((-1,) + (1,) * (len(shape) - 1 - axis_at))
    return factor_of


def centred(key, shape, width, most, cuts=(), held_as=jnp.bfloat16):
    drawn = jax.random.normal(key, shape, jnp.float32) * width
    if len(cuts) > 0:
        drawn = steps_of(key, shape, cuts, -0.22, 0.18) * drawn
    return jnp.clip(drawn, min=-most, max=most).astype(held_as)


def setup_inputs(seed: int = 0) -> dict:
    splits = jax.random.split(jax.random.key(seed), 7)
    return {
        "src_points": centred(splits[0], (RC, DIM, PTS), 0.25, 1.5, ((0, 8), (1, 4))),
        "dst_points": centred(splits[1], (CC, DIM, PTS), 0.25, 1.5, ((0, 4), (1, 8))),
        "support": draw_support(jax.random.fold_in(splits[6], 71), 0),
        "log_src_mass": jnp.clip(jax.random.uniform(splits[3], (RC, PTS), jnp.float32, -1.0, 1.0) * steps_of(splits[3], (RC, PTS), ((0, 8),), -0.4, 0.0), -1.0, 1.0),
        "log_dst_mass": jnp.clip(jax.random.uniform(splits[4], (CC, PTS), jnp.float32, -1.0, 1.0) * steps_of(splits[4], (CC, PTS), ((0, 4),), -0.4, 0.0), -1.0, 1.0),
        "dst_potential": draw_dst_potential(jax.random.fold_in(splits[6], 71), 0),
    }


blur_scale = 0.5
floor_value = -1.0e30


def square_norms(points):
    values = points.astype(jnp.float32)
    return jnp.sum(values * values, axis=-2)


def block_costs(src_tile, dst_tiles, src_sq, dst_sq):
    inner_prod = jnp.einsum("dp,kdq->kpq", src_tile.astype(jnp.float32), dst_tiles.astype(jnp.float32))
    return src_sq[None, :, None] + dst_sq[:, None, :] - 2.0 * inner_prod


def reference(src_points, dst_points, support, log_src_mass, log_dst_mass, dst_potential):
    src_sq = square_norms(src_points)
    dst_sq = square_norms(dst_points)

    def row_half(inputs):
        src_tile, tile_sq, chosen, log_mass = inputs
        costs = block_costs(src_tile, dst_points[chosen], tile_sq, dst_sq[chosen])
        scores = (dst_potential[chosen][:, None, :] - costs) / blur_scale
        highest = jnp.max(scores, axis=(0, 2))
        totals = jnp.sum(jnp.exp(scores - highest[None, :, None]), axis=(0, 2))
        return blur_scale * (log_mass - (highest + jnp.log(totals)))

    src_new = lax.map(row_half, (src_points, src_sq, support, log_src_mass))

    def col_half(running, inputs):
        col_high, col_total = running
        src_tile, tile_sq, chosen, row_pot = inputs
        costs = block_costs(src_tile, dst_points[chosen], tile_sq, dst_sq[chosen])
        scores = (row_pot[None, :, None] - costs) / blur_scale
        tile_high = jnp.max(scores, axis=1)
        tile_total = jnp.sum(jnp.exp(scores - tile_high[:, None, :]), axis=1)
        old_high = col_high[chosen]
        old_total = col_total[chosen]
        new_high = jnp.maximum(old_high, tile_high)
        new_total = old_total * jnp.exp(old_high - new_high) + tile_total * jnp.exp(tile_high - new_high)
        return (col_high.at[chosen].set(new_high), col_total.at[chosen].set(new_total)), None

    start_high = jnp.full(dst_potential.shape, floor_value, jnp.float32)
    start_total = jnp.zeros(dst_potential.shape, jnp.float32)
    (col_high, col_total), unused = lax.scan(col_half, (start_high, start_total), (src_points, src_sq, support, src_new))
    dst_new = blur_scale * (log_dst_mass - (col_high + jnp.log(col_total)))
    return (src_new, dst_new)
```

```python
import functools

import jax
import jax.numpy as jnp
from jax import lax
from jax.experimental import pallas as pl
from jax.experimental.pallas import tpu as pltpu
from jax.sharding import PartitionSpec as P

blur_scale = 0.5
floor_value = -1e30
row_low, row_top = 1e-6, 1e30
col_low, col_top = 1e-20, 1e20
AUG = 80
ROWS = 256
COLS = 256


def tile_kernel(
    per_dev, sup_ref, x_ref, y_ref, g_ref, mass_ref, src_ref, t_ref, yaug, xt, ebuf, acc
):
    cc, dim, pts = y_ref.shape
    per_row = sup_ref.shape[1]
    first = lax.axis_index("col") * per_dev

    def prep(b, carry):
        y = y_ref[b]
        yf = y.astype(jnp.float32)
        sq = jnp.sum(yf * yf, axis=0, keepdims=True)
        bias = 2.0 * (g_ref[pl.ds(b, 1), :] - sq)
        hi = bias.astype(jnp.bfloat16).astype(jnp.float32)
        rest = bias - hi
        mid = rest.astype(jnp.bfloat16).astype(jnp.float32)
        lo = rest - mid
        at = lax.broadcasted_iota(jnp.int32, (AUG - dim, pts), 0)
        extra = jnp.where(at == 0, hi, jnp.where(at == 1, mid, jnp.where(at == 2, lo, 0.0)))
        yaug[b, :dim, :] = y
        yaug[b, dim:, :] = extra.astype(jnp.bfloat16)
        return carry

    lax.fori_loop(0, cc, prep, 0)
    t_ref[...] = jnp.zeros_like(t_ref)

    def cluster(a, carry):
        xf = x_ref[a].astype(jnp.float32)
        x_sq = jnp.sum(xf * xf, axis=0, keepdims=True)
        at = lax.broadcasted_iota(jnp.int32, (128 - dim, pts), 0)
        whole = jnp.concatenate([xf * 4.0, jnp.where(at < 3, 1.0, 0.0)], axis=0)
        xt[...] = whole.T.astype(jnp.bfloat16)
        acc[...] = jnp.zeros_like(acc)

        def block(k, carry):
            b = sup_ref[first + a, k]
            for n in range(pts // COLS):
                y = yaug[b, :, n * COLS : (n + 1) * COLS]
                for m in range(pts // ROWS):
                    rows = pl.ds(m * ROWS, ROWS)
                    p = jnp.dot(xt[rows, :AUG], y, preferred_element_type=jnp.float32)
                    e = jnp.exp(p)
                    part = e[:, :128]
                    for q in range(1, COLS // 128):
                        part = part + e[:, q * 128 : (q + 1) * 128]
                    acc[rows, :] += part
                    ebuf[k, rows, n * COLS : (n + 1) * COLS] = e.astype(jnp.bfloat16)
            return carry

        lax.fori_loop(0, per_row, block, 0)
        total = jnp.sum(acc[...].T, axis=0, keepdims=True)
        mass = mass_ref[pl.ds(first + a, 1), :]
        src_ref[pl.ds(a, 1), :] = blur_scale * (mass + 2.0 * x_sq - jnp.log(total))
        fine = (total >= row_low) & (total <= row_top)
        w = jnp.where(fine, jnp.exp(mass) / total, jnp.nan)
        w_hi = w.astype(jnp.bfloat16).astype(jnp.float32)
        at16 = lax.broadcasted_iota(jnp.int32, (16, pts), 0)
        w16 = jnp.where(at16 == 0, w_hi, jnp.where(at16 == 1, w - w_hi, 0.0)).astype(jnp.bfloat16)

        def column(k, carry):
            b = sup_ref[first + a, k]
            got = jnp.dot(w16, ebuf[k], preferred_element_type=jnp.float32)
            t_ref[pl.ds(b, 1), :] += got[0:1] + got[1:2]
            return carry

        lax.fori_loop(0, per_row, column, 0)
        return carry

    lax.fori_loop(0, per_dev, cluster, 0)


def tiles(per_dev, support, x_mine, y_all, g_all, log_src_mass):
    cc, dim, pts = y_all.shape
    per_row = support.shape[1]
    vmem = pl.BlockSpec(memory_space=pltpu.VMEM)
    return pl.pallas_call(
        functools.partial(tile_kernel, per_dev),
        out_shape=(
            jax.ShapeDtypeStruct((per_dev, pts), jnp.float32),
            jax.ShapeDtypeStruct((cc, pts), jnp.float32),
        ),
        in_specs=[pl.BlockSpec(memory_space=pltpu.SMEM), vmem, vmem, vmem, vmem],
        out_specs=(vmem, vmem),
        scratch_shapes=[
            pltpu.VMEM((cc, AUG, pts), jnp.bfloat16),
            pltpu.VMEM((pts, 128), jnp.bfloat16),
            pltpu.VMEM((per_row, pts, pts), jnp.bfloat16),
            pltpu.VMEM((pts, 128), jnp.float32),
        ],
        compiler_params=pltpu.CompilerParams(vmem_limit_bytes=56 * 1024 * 1024),
        name="tiles",
    )(support, x_mine, y_all, g_all, log_src_mass)


def exact_path(per_dev, support, x_mine, y_all, g_all, log_src_mass, log_dst_mass):
    cc, dim, pts = y_all.shape
    per_row = support.shape[1]
    first = lax.axis_index("col") * per_dev
    chosen = lax.dynamic_slice_in_dim(support, first, per_dev, 0)
    mass = lax.dynamic_slice_in_dim(log_src_mass, first, per_dev, 0)

    def scores_of(a, b):
        x = lax.dynamic_index_in_dim(x_mine, a, 0, keepdims=False)
        y = lax.dynamic_index_in_dim(y_all, b, 0, keepdims=False)
        xf, yf = x.astype(jnp.float32), y.astype(jnp.float32)
        inner = lax.dot_general(x, y, (((0,), (0,)), ((), ())), preferred_element_type=jnp.float32)
        return jnp.sum(xf * xf, 0)[:, None] + jnp.sum(yf * yf, 0)[None, :] - 2.0 * inner

    def row_turn(t, running):
        high, total = running
        a, b = t // per_row, chosen[t // per_row, t % per_row]
        s = (g_all[b][None, :] - scores_of(a, b)) / blur_scale
        new_high = jnp.maximum(high[a], jnp.max(s, axis=1))
        new_total = total[a] * jnp.exp(high[a] - new_high) + jnp.sum(
            jnp.exp(s - new_high[:, None]), axis=1
        )
        return high.at[a].set(new_high), total.at[a].set(new_total)

    start = (jnp.full((per_dev, pts), floor_value), jnp.zeros((per_dev, pts)))
    high, total = lax.fori_loop(0, per_dev * per_row, row_turn, start)
    src_mine = blur_scale * (mass - (high + jnp.log(total)))

    def col_turn(t, running):
        high, total = running
        a, b = t // per_row, chosen[t // per_row, t % per_row]
        s = (src_mine[a][:, None] - scores_of(a, b)) / blur_scale
        new_high = jnp.maximum(high[b], jnp.max(s, axis=0))
        new_total = total[b] * jnp.exp(high[b] - new_high) + jnp.sum(
            jnp.exp(s - new_high[None, :]), axis=0
        )
        return high.at[b].set(new_high), total.at[b].set(new_total)

    start = (jnp.full((cc, pts), floor_value), jnp.zeros((cc, pts)))
    high, total = lax.fori_loop(0, per_dev * per_row, col_turn, start)
    top = lax.pmax(high, ("row", "col"))
    total = lax.psum(total * jnp.exp(high - top), ("row", "col"))
    count = log_dst_mass.shape[0]
    last = lax.dynamic_slice_in_dim(top + jnp.log(total), lax.axis_index("col") * count, count, 0)
    return lax.all_gather(src_mine, "col", axis=0, tiled=True), blur_scale * (log_dst_mass - last)


def body(n_col, src_points, dst_points, support, log_src_mass, log_dst_mass, dst_potential):
    per_dev = support.shape[0] // n_col
    count = dst_points.shape[0]
    x_mine = lax.all_to_all(src_points, "col", split_axis=0, concat_axis=1, tiled=True)
    y_some = lax.all_gather(dst_points, "row", axis=1, tiled=True)
    y_all = lax.all_gather(y_some, "col", axis=0, tiled=True)
    g_all = lax.all_gather(dst_potential, "col", axis=0, tiled=True)
    src_mine, part = tiles(per_dev, support, x_mine, y_all, g_all, log_src_mass)
    whole = lax.psum(part, ("row", "col"))
    src_new = lax.all_gather(src_mine, "col", axis=0, tiled=True)
    fine = jnp.all((whole >= col_low) & (whole <= col_top))
    mine = lax.dynamic_slice_in_dim(whole, lax.axis_index("col") * count, count, 0)
    dst_new = blur_scale * (log_dst_mass - (jnp.log(mine) - 2.0 * dst_potential))
    return lax.cond(
        fine,
        lambda: (src_new, dst_new),
        lambda: exact_path(
            per_dev, support, x_mine, y_all, g_all, log_src_mass, log_dst_mass
        ),
    )


def solution(mesh):
    return jax.shard_map(
        functools.partial(body, mesh.shape["col"]),
        mesh=mesh,
        in_specs=(
            P("row", "col", None),
            P("col", "row", None),
            P("row", None),
            P("row", None),
            P("col", None),
            P("col", None),
        ),
        out_specs=(P("row", None), P("col", None)),
        check_vma=False,
    )
```

```python
import functools

import jax
import jax.numpy as jnp
from jax import lax
from jax.experimental import pallas as pl
from jax.experimental.pallas import tpu as pltpu
from jax.sharding import PartitionSpec as P

blur_scale = 0.5
floor_value = -1e30
row_low, row_top = 1e-6, 1e30
col_low, col_top = 1e-20, 1e20
AUG = 80
ROWS = 256
COLS = 256


def tile_kernel(
    per_dev, sup_ref, x_ref, y_ref, g_ref, mass_ref, src_ref, t_ref, yaug, xt, ebuf, acc
):
    n_col, n_row, count, share, pts = y_ref.shape
    dim = n_row * share
    per_row = sup_ref.shape[1]
    first = lax.axis_index("col") * per_dev

    def prep(b, carry):
        yf = jnp.concatenate(
            [y_ref[b // count, r, b % count].astype(jnp.float32) for r in range(n_row)], axis=0
        )
        y = yf.astype(jnp.bfloat16)
        sq = jnp.sum(yf * yf, axis=0, keepdims=True)
        bias = 2.0 * (g_ref[b // count, pl.ds(b % count, 1), :] - sq)
        hi = bias.astype(jnp.bfloat16).astype(jnp.float32)
        rest = bias - hi
        mid = rest.astype(jnp.bfloat16).astype(jnp.float32)
        lo = rest - mid
        at = lax.broadcasted_iota(jnp.int32, (AUG - dim, pts), 0)
        extra = jnp.where(at == 0, hi, jnp.where(at == 1, mid, jnp.where(at == 2, lo, 0.0)))
        yaug[b, :dim, :] = y
        yaug[b, dim:, :] = extra.astype(jnp.bfloat16)
        return carry

    lax.fori_loop(0, n_col * count, prep, 0)
    t_ref[...] = jnp.zeros_like(t_ref)

    def cluster(a, carry):
        xf = jnp.concatenate(
            [x_ref[c, a].astype(jnp.float32) for c in range(n_col)], axis=0
        )
        x_sq = jnp.sum(xf * xf, axis=0, keepdims=True)
        at = lax.broadcasted_iota(jnp.int32, (128 - dim, pts), 0)
        whole = jnp.concatenate([xf * 4.0, jnp.where(at < 3, 1.0, 0.0)], axis=0)
        xt[...] = whole.T.astype(jnp.bfloat16)
        acc[...] = jnp.zeros_like(acc)

        def block(k, carry):
            b = sup_ref[first + a, k]
            for n in range(pts // COLS):
                y = yaug[b, :, n * COLS : (n + 1) * COLS]
                for m in range(pts // ROWS):
                    rows = pl.ds(m * ROWS, ROWS)
                    p = jnp.dot(xt[rows, :AUG], y, preferred_element_type=jnp.float32)
                    e = jnp.exp(p)
                    part = e[:, :128]
                    for q in range(1, COLS // 128):
                        part = part + e[:, q * 128 : (q + 1) * 128]
                    acc[rows, :] += part
                    ebuf[k, rows, n * COLS : (n + 1) * COLS] = e.astype(jnp.bfloat16)
            return carry

        lax.fori_loop(0, per_row, block, 0)
        total = jnp.sum(acc[...].T, axis=0, keepdims=True)
        mass = mass_ref[pl.ds(first + a, 1), :]
        src_ref[pl.ds(a, 1), :] = blur_scale * (mass + 2.0 * x_sq - jnp.log(total))
        fine = (total >= row_low) & (total <= row_top)
        w = jnp.where(fine, jnp.exp(mass) / total, jnp.nan)
        w_hi = w.astype(jnp.bfloat16).astype(jnp.float32)
        at16 = lax.broadcasted_iota(jnp.int32, (16, pts), 0)
        w16 = jnp.where(at16 == 0, w_hi, jnp.where(at16 == 1, w - w_hi, 0.0)).astype(jnp.bfloat16)

        def column(k, carry):
            b = sup_ref[first + a, k]
            got = jnp.dot(w16, ebuf[k], preferred_element_type=jnp.float32)
            t_ref[b // count, pl.ds(b % count, 1), :] += got[0:1] + got[1:2]
            return carry

        lax.fori_loop(0, per_row, column, 0)
        return carry

    lax.fori_loop(0, per_dev, cluster, 0)


def tiles(per_dev, support, x_mine, y_all, g_all, log_src_mass):
    n_col, n_row, count, share, pts = y_all.shape
    per_row = support.shape[1]
    vmem = pl.BlockSpec(memory_space=pltpu.VMEM)
    return pl.pallas_call(
        functools.partial(tile_kernel, per_dev),
        out_shape=(
            jax.ShapeDtypeStruct((per_dev, pts), jnp.float32),
            jax.ShapeDtypeStruct((n_col, count, pts), jnp.float32),
        ),
        in_specs=[pl.BlockSpec(memory_space=pltpu.SMEM), vmem, vmem, vmem, vmem],
        out_specs=(vmem, vmem),
        scratch_shapes=[
            pltpu.VMEM((n_col * count, AUG, pts), jnp.bfloat16),
            pltpu.VMEM((pts, 128), jnp.bfloat16),
            pltpu.VMEM((per_row, pts, pts), jnp.bfloat16),
            pltpu.VMEM((pts, 128), jnp.float32),
        ],
        compiler_params=pltpu.CompilerParams(vmem_limit_bytes=56 * 1024 * 1024),
        name="tiles",
    )(support, x_mine, y_all, g_all, log_src_mass)


def exact_path(per_dev, support, x_mine, y_all, g_all, log_src_mass, log_dst_mass):
    n_col, n_row, count, share, pts = y_all.shape
    cc, dim = n_col * count, n_row * share
    x_mine = x_mine.transpose(1, 0, 2, 3).reshape(per_dev, dim, pts)
    y_all = y_all.transpose(0, 2, 1, 3, 4).reshape(cc, dim, pts)
    g_all = g_all.reshape(cc, pts)
    per_row = support.shape[1]
    first = lax.axis_index("col") * per_dev
    chosen = lax.dynamic_slice_in_dim(support, first, per_dev, 0)
    mass = lax.dynamic_slice_in_dim(log_src_mass, first, per_dev, 0)

    def scores_of(a, b):
        x = lax.dynamic_index_in_dim(x_mine, a, 0, keepdims=False)
        y = lax.dynamic_index_in_dim(y_all, b, 0, keepdims=False)
        xf, yf = x.astype(jnp.float32), y.astype(jnp.float32)
        inner = lax.dot_general(x, y, (((0,), (0,)), ((), ())), preferred_element_type=jnp.float32)
        return jnp.sum(xf * xf, 0)[:, None] + jnp.sum(yf * yf, 0)[None, :] - 2.0 * inner

    def row_turn(t, running):
        high, total = running
        a, b = t // per_row, chosen[t // per_row, t % per_row]
        s = (g_all[b][None, :] - scores_of(a, b)) / blur_scale
        new_high = jnp.maximum(high[a], jnp.max(s, axis=1))
        new_total = total[a] * jnp.exp(high[a] - new_high) + jnp.sum(
            jnp.exp(s - new_high[:, None]), axis=1
        )
        return high.at[a].set(new_high), total.at[a].set(new_total)

    start = (jnp.full((per_dev, pts), floor_value), jnp.zeros((per_dev, pts)))
    high, total = lax.fori_loop(0, per_dev * per_row, row_turn, start)
    src_mine = blur_scale * (mass - (high + jnp.log(total)))

    def col_turn(t, running):
        high, total = running
        a, b = t // per_row, chosen[t // per_row, t % per_row]
        s = (src_mine[a][:, None] - scores_of(a, b)) / blur_scale
        new_high = jnp.maximum(high[b], jnp.max(s, axis=0))
        new_total = total[b] * jnp.exp(high[b] - new_high) + jnp.sum(
            jnp.exp(s - new_high[None, :]), axis=0
        )
        return high.at[b].set(new_high), total.at[b].set(new_total)

    start = (jnp.full((cc, pts), floor_value), jnp.zeros((cc, pts)))
    high, total = lax.fori_loop(0, per_dev * per_row, col_turn, start)
    top = lax.pmax(high, ("row", "col"))
    total = lax.psum(total * jnp.exp(high - top), ("row", "col"))
    last = lax.dynamic_slice_in_dim(top + jnp.log(total), lax.axis_index("col") * count, count, 0)
    return lax.all_gather(src_mine, "col", axis=0, tiled=True), blur_scale * (log_dst_mass - last)


def remote(src, dst, send, recv, row, col):
    return pltpu.make_async_remote_copy(
        src_ref=src,
        dst_ref=dst,
        send_sem=send,
        recv_sem=recv,
        device_id=(row, col),
        device_id_type=pl.DeviceIdType.MESH,
    )


def greet(n_row, n_col, row, col):
    barrier = pltpu.get_barrier_semaphore()
    for j in range(1, n_row):
        pl.semaphore_signal(
            barrier,
            inc=1,
            device_id=(lax.rem(row + j, n_row), col),
            device_id_type=pl.DeviceIdType.MESH,
        )
    for j in range(1, n_col):
        pl.semaphore_signal(
            barrier,
            inc=1,
            device_id=(row, lax.rem(col + j, n_col)),
            device_id_type=pl.DeviceIdType.MESH,
        )
    pl.semaphore_wait(barrier, n_row + n_col - 2)


def spread_kernel(
    src_ref, dst_ref, pot_ref, x_ref, y_ref, g_ref, own, x_send, x_recv, g_send, g_recv,
    row_send, y_send, pair_send, y_recv,
):
    n_col, n_row = y_ref.shape[:2]
    per_dev = x_ref.shape[1]
    n_y = n_col // 2
    row, col = lax.axis_index("row"), lax.axis_index("col")
    pair = col + 1 - 2 * lax.rem(col, 2)
    kept = (
        pltpu.make_async_copy(dst_ref, y_ref.at[col, row], own.at[0]),
        pltpu.make_async_copy(
            src_ref.at[pl.ds(col * per_dev, per_dev)], x_ref.at[col], own.at[1]
        ),
        pltpu.make_async_copy(pot_ref, g_ref.at[col], own.at[2]),
    )
    for copy in kept:
        copy.start()
    greet(n_row, n_col, row, col)

    def to_row(j):
        there = lax.rem(row + j, n_row)
        return remote(
            dst_ref, y_ref.at[col, row], row_send.at[j], y_recv.at[col, row], there, col
        )

    def to_y(i, dy):
        at = lax.rem(row + n_row - i, n_row)
        block = y_ref.at[col, at]
        there = lax.rem(col + 2 * dy, n_col)
        return remote(block, block, y_send.at[dy, i], y_recv.at[col, at], row, there)

    def to_pair(i, dy):
        at = lax.rem(row + n_row - i, n_row)
        origin = lax.rem(col + n_col - 2 * dy, n_col)
        block = y_ref.at[origin, at]
        return remote(block, block, pair_send.at[dy, i], y_recv.at[origin, at], row, pair)

    def arrived(origin, at):
        block = y_ref.at[origin, at]
        remote(block, block, row_send.at[0], y_recv.at[origin, at], row, pair).wait_recv()

    def to_col(j):
        there = lax.rem(col + j, n_col)
        return (
            remote(
                src_ref.at[pl.ds(there * per_dev, per_dev)],
                x_ref.at[col], x_send.at[j], x_recv.at[col], row, there,
            ),
            remote(pot_ref, g_ref.at[col], g_send.at[j], g_recv.at[col], row, there),
        )

    for j in range(1, n_row):
        to_row(j).start()
    kept[0].wait()
    for dy in range(1, n_y):
        to_y(0, dy).start()
    to_pair(0, 0).start()
    for j in range(1, n_col):
        for copy in to_col(j):
            copy.start()

    def hand_on(i):
        at = lax.rem(row + n_row - i, n_row)
        for dy in range(1, n_y):
            arrived(lax.rem(col + n_col - 2 * dy, n_col), at)
            to_pair(i, dy).start()

    def step(i, carry):
        arrived(col, lax.rem(row + n_row - i, n_row))
        for dy in range(1, n_y):
            to_y(i, dy).start()
        to_pair(i, 0).start()
        hand_on(i - 1)
        return carry

    lax.fori_loop(1, n_row, step, 0)
    hand_on(n_row - 1)

    def finish(i, carry):
        for dy in range(n_y):
            arrived(lax.rem(pair + 2 * dy, n_col), i)
            to_pair(i, dy).wait_send()
            if dy > 0:
                to_y(i, dy).wait_send()
        return carry

    lax.fori_loop(0, n_row, finish, 0)
    for j in range(1, n_row):
        to_row(j).wait_send()
    for j in range(1, n_col):
        for copy in to_col(j):
            copy.wait_send()
        origin = lax.rem(col + j, n_col)
        remote(
            x_ref.at[origin], x_ref.at[origin], x_send.at[j], x_recv.at[origin], row, pair
        ).wait_recv()
        remote(
            g_ref.at[origin], g_ref.at[origin], g_send.at[j], g_recv.at[origin], row, pair
        ).wait_recv()
    kept[1].wait()
    kept[2].wait()


def spread(n_row, n_col, src_points, dst_points, dst_potential):
    sources, dims, pts = src_points.shape
    per_dev = sources // n_col
    sem = pltpu.SemaphoreType.DMA
    anywhere = pl.BlockSpec(memory_space=pl.ANY)
    return pl.pallas_call(
        spread_kernel,
        out_shape=(
            jax.ShapeDtypeStruct((n_col, per_dev, dims, pts), src_points.dtype),
            jax.ShapeDtypeStruct((n_col, n_row) + dst_points.shape, dst_points.dtype),
            jax.ShapeDtypeStruct((n_col,) + dst_potential.shape, jnp.float32),
        ),
        in_specs=[anywhere] * 3,
        out_specs=(anywhere,) * 3,
        scratch_shapes=[
            sem((3,)),
            sem((n_col,)),
            sem((n_col,)),
            sem((n_col,)),
            sem((n_col,)),
            sem((n_row,)),
            sem((n_col // 2, n_row)),
            sem((n_col // 2, n_row)),
            sem((n_col, n_row)),
        ],
        compiler_params=pltpu.CompilerParams(collective_id=0, has_side_effects=True),
        name="spread",
    )(src_points, dst_points, dst_potential)


def merge_kernel(
    part_ref, src_ref, mass_ref, pot_ref, new_src, new_dst, bad_ref, by_col, by_row, srcs, bads,
    part_send, part_recv, src_send, src_recv, row_send, row_recv, bad_send, bad_recv,
):
    n_col = by_col.shape[0]
    n_row = by_row.shape[0]
    per_dev = src_ref.shape[0]
    row, col = lax.axis_index("row"), lax.axis_index("col")
    greet(n_row, n_col, row, col)
    started = []
    for j in range(1, n_col):
        there = lax.rem(col + j, n_col)
        started.append(
            remote(
                part_ref.at[there], by_col.at[col], part_send.at[j], part_recv.at[col], row, there
            )
        )
        started[-1].start()
    for j in range(1, n_col):
        there = lax.rem(col + j, n_col)
        started.append(
            remote(src_ref, srcs.at[col], src_send.at[j], src_recv.at[col], row, there)
        )
        started[-1].start()
    by_col[col] = part_ref[col]
    srcs[col] = src_ref[...]

    def arrivals(held, sems, me, count):
        for j in range(1, count):
            at = lax.rem(me + j, count)
            near = lax.rem(col + 1, n_col)
            remote(held.at[at], held.at[at], bad_send.at[0], sems.at[at], row, near).wait_recv()

    arrivals(by_col, part_recv, col, n_col)
    total = by_col[0]
    for c in range(1, n_col):
        total = total + by_col[c]
    by_row[row] = total
    for j in range(1, n_row):
        there = lax.rem(row + j, n_row)
        block = by_row.at[row]
        started.append(remote(block, block, row_send.at[j], row_recv.at[row], there, col))
        started[-1].start()
    arrivals(srcs, src_recv, col, n_col)
    for c in range(n_col):
        new_src[c * per_dev : (c + 1) * per_dev, :] = srcs[c]
    arrivals(by_row, row_recv, row, n_row)
    total = by_row[0]
    for r in range(1, n_row):
        total = total + by_row[r]
    bad = jnp.where((total >= col_low) & (total <= col_top), 0.0, 1.0)
    bad = jnp.max(jnp.max(bad, axis=1, keepdims=True), axis=0, keepdims=True)
    bads[col] = jnp.broadcast_to(bad, bads.shape[1:])
    for j in range(1, n_col):
        there = lax.rem(col + j, n_col)
        block = bads.at[col]
        started.append(remote(block, block, bad_send.at[j], bad_recv.at[col], row, there))
        started[-1].start()
    new_dst[...] = blur_scale * (mass_ref[...] - (jnp.log(total) - 2.0 * pot_ref[...]))
    arrivals(bads, bad_recv, col, n_col)
    worst = bads[0]
    for c in range(1, n_col):
        worst = jnp.maximum(worst, bads[c])
    bad_ref[...] = worst
    for copy in started:
        copy.wait_send()


def merge(n_row, part, src_mine, log_dst_mass, dst_potential):
    n_col, count, pts = part.shape
    per_dev = src_mine.shape[0]
    sem = pltpu.SemaphoreType.DMA
    vmem = pl.BlockSpec(memory_space=pltpu.VMEM)
    return pl.pallas_call(
        merge_kernel,
        out_shape=(
            jax.ShapeDtypeStruct((n_col * per_dev, pts), jnp.float32),
            jax.ShapeDtypeStruct((count, pts), jnp.float32),
            jax.ShapeDtypeStruct((8, 128), jnp.float32),
        ),
        in_specs=[vmem] * 4,
        out_specs=(vmem,) * 3,
        scratch_shapes=[
            pltpu.VMEM((n_col, count, pts), jnp.float32),
            pltpu.VMEM((n_row, count, pts), jnp.float32),
            pltpu.VMEM((n_col, per_dev, pts), jnp.float32),
            pltpu.VMEM((n_col, 8, 128), jnp.float32),
            sem((n_col,)),
            sem((n_col,)),
            sem((n_col,)),
            sem((n_col,)),
            sem((n_row,)),
            sem((n_row,)),
            sem((n_col,)),
            sem((n_col,)),
        ],
        compiler_params=pltpu.CompilerParams(collective_id=1, has_side_effects=True),
        name="merge",
    )(part, src_mine, log_dst_mass, dst_potential)


def body(n_row, n_col, src_points, dst_points, support, log_src_mass, log_dst_mass, dst_potential):
    per_dev = support.shape[0] // n_col
    x_mine, y_all, g_all = spread(n_row, n_col, src_points, dst_points, dst_potential)
    src_mine, part = tiles(per_dev, support, x_mine, y_all, g_all, log_src_mass)
    src_new, dst_new, bad = merge(n_row, part, src_mine, log_dst_mass, dst_potential)
    return lax.cond(
        bad[0, 0] < 0.5,
        lambda: (src_new, dst_new),
        lambda: exact_path(
            per_dev, support, x_mine, y_all, g_all, log_src_mass, log_dst_mass
        ),
    )


def solution(mesh):
    return jax.shard_map(
        functools.partial(body, mesh.shape["row"], mesh.shape["col"]),
        mesh=mesh,
        in_specs=(
            P("row", "col", None),
            P("col", "row", None),
            P("row", None),
            P("row", None),
            P("col", None),
            P("col", None),
        ),
        out_specs=(P("row", None), P("col", None)),
        check_vma=False,
    )
```

```python
import functools

import jax
import jax.numpy as jnp
from jax import lax
from jax.experimental import pallas as pl
from jax.experimental.pallas import tpu as pltpu
from jax.sharding import PartitionSpec as P

blur_scale = 0.5
floor_value = -1e30
row_low, row_top = 1e-6, 1e30
col_low, col_top = 1e-20, 1e20
AUG = 80
ROWS = 256
COLS = 256


def tile_kernel(
    per_dev, sup_ref, x_ref, y_ref, g_ref, mass_ref, src_ref, t_ref, yaug, xt, ebuf, acc, wbuf
):
    n_col, n_row, count, share, pts = y_ref.shape
    dim = n_row * share
    per_row = sup_ref.shape[1]
    first = lax.axis_index("col") * per_dev

    def prep(b, carry):
        yf = jnp.concatenate(
            [y_ref[b // count, r, b % count].astype(jnp.float32) for r in range(n_row)], axis=0
        )
        y = yf.astype(jnp.bfloat16)
        sq = jnp.sum(yf * yf, axis=0, keepdims=True)
        bias = 2.0 * (g_ref[b // count, pl.ds(b % count, 1), :] - sq)
        hi = bias.astype(jnp.bfloat16).astype(jnp.float32)
        rest = bias - hi
        mid = rest.astype(jnp.bfloat16).astype(jnp.float32)
        lo = rest - mid
        at = lax.broadcasted_iota(jnp.int32, (AUG - dim, pts), 0)
        extra = jnp.where(at == 0, hi, jnp.where(at == 1, mid, jnp.where(at == 2, lo, 0.0)))
        yaug[b, :dim, :] = y
        yaug[b, dim:, :] = extra.astype(jnp.bfloat16)
        return carry

    lax.fori_loop(0, n_col * count, prep, 0)
    t_ref[...] = jnp.zeros_like(t_ref)

    def add_column(a, k, n):
        b = sup_ref[first + a, k]
        cols = slice(n * COLS, (n + 1) * COLS)
        got = jnp.dot(wbuf[...], ebuf[k, :, cols], preferred_element_type=jnp.float32)
        t_ref[b // count, pl.ds(b % count, 1), cols] += got[0:1] + got[1:2]

    def cluster(a, carry, after=True):
        xf = jnp.concatenate(
            [x_ref[c, a].astype(jnp.float32) for c in range(n_col)], axis=0
        )
        x_sq = jnp.sum(xf * xf, axis=0, keepdims=True)
        at = lax.broadcasted_iota(jnp.int32, (128 - dim, pts), 0)
        whole = jnp.concatenate([xf * 4.0, jnp.where(at < 3, 1.0, 0.0)], axis=0)
        xt[...] = whole.T.astype(jnp.bfloat16)
        acc[...] = jnp.zeros_like(acc)

        def block(k, carry):
            b = sup_ref[first + a, k]
            for n in range(pts // COLS):
                if after:
                    add_column(a - 1, k, n)
                y = yaug[b, :, n * COLS : (n + 1) * COLS]
                for m in range(pts // ROWS):
                    rows = pl.ds(m * ROWS, ROWS)
                    p = jnp.dot(xt[rows, :AUG], y, preferred_element_type=jnp.float32)
                    e = jnp.exp(p)
                    part = e[:, :128]
                    for q in range(1, COLS // 128):
                        part = part + e[:, q * 128 : (q + 1) * 128]
                    acc[rows, :] += part
                    ebuf[k, rows, n * COLS : (n + 1) * COLS] = e.astype(jnp.bfloat16)
            return carry

        lax.fori_loop(0, per_row, block, 0)
        total = jnp.sum(acc[...].T, axis=0, keepdims=True)
        mass = mass_ref[pl.ds(first + a, 1), :]
        src_ref[pl.ds(a, 1), :] = blur_scale * (mass + 2.0 * x_sq - jnp.log(total))
        fine = (total >= row_low) & (total <= row_top)
        w = jnp.where(fine, jnp.exp(mass) / total, jnp.nan)
        w_hi = w.astype(jnp.bfloat16).astype(jnp.float32)
        at16 = lax.broadcasted_iota(jnp.int32, (16, pts), 0)
        w16 = jnp.where(at16 == 0, w_hi, jnp.where(at16 == 1, w - w_hi, 0.0))
        wbuf[...] = w16.astype(jnp.bfloat16)
        return carry

    cluster(0, 0, after=False)
    lax.fori_loop(1, per_dev, cluster, 0)

    def column(k, carry):
        for n in range(pts // COLS):
            add_column(per_dev - 1, k, n)
        return carry

    lax.fori_loop(0, per_row, column, 0)


def tiles(per_dev, support, x_mine, y_all, g_all, log_src_mass):
    n_col, n_row, count, share, pts = y_all.shape
    per_row = support.shape[1]
    vmem = pl.BlockSpec(memory_space=pltpu.VMEM)
    return pl.pallas_call(
        functools.partial(tile_kernel, per_dev),
        out_shape=(
            jax.ShapeDtypeStruct((per_dev, pts), jnp.float32),
            jax.ShapeDtypeStruct((n_col, count, pts), jnp.float32),
        ),
        in_specs=[pl.BlockSpec(memory_space=pltpu.SMEM), vmem, vmem, vmem, vmem],
        out_specs=(vmem, vmem),
        scratch_shapes=[
            pltpu.VMEM((n_col * count, AUG, pts), jnp.bfloat16),
            pltpu.VMEM((pts, 128), jnp.bfloat16),
            pltpu.VMEM((per_row, pts, pts), jnp.bfloat16),
            pltpu.VMEM((pts, 128), jnp.float32),
            pltpu.VMEM((16, pts), jnp.bfloat16),
        ],
        compiler_params=pltpu.CompilerParams(vmem_limit_bytes=56 * 1024 * 1024),
        name="tiles",
    )(support, x_mine, y_all, g_all, log_src_mass)


def exact_path(per_dev, support, x_mine, y_all, g_all, log_src_mass, log_dst_mass):
    n_col, n_row, count, share, pts = y_all.shape
    cc, dim = n_col * count, n_row * share
    x_mine = x_mine.transpose(1, 0, 2, 3).reshape(per_dev, dim, pts)
    y_all = y_all.transpose(0, 2, 1, 3, 4).reshape(cc, dim, pts)
    g_all = g_all.reshape(cc, pts)
    per_row = support.shape[1]
    first = lax.axis_index("col") * per_dev
    chosen = lax.dynamic_slice_in_dim(support, first, per_dev, 0)
    mass = lax.dynamic_slice_in_dim(log_src_mass, first, per_dev, 0)

    def scores_of(a, b):
        x = lax.dynamic_index_in_dim(x_mine, a, 0, keepdims=False)
        y = lax.dynamic_index_in_dim(y_all, b, 0, keepdims=False)
        xf, yf = x.astype(jnp.float32), y.astype(jnp.float32)
        inner = lax.dot_general(x, y, (((0,), (0,)), ((), ())), preferred_element_type=jnp.float32)
        return jnp.sum(xf * xf, 0)[:, None] + jnp.sum(yf * yf, 0)[None, :] - 2.0 * inner

    def row_turn(t, running):
        high, total = running
        a, b = t // per_row, chosen[t // per_row, t % per_row]
        s = (g_all[b][None, :] - scores_of(a, b)) / blur_scale
        new_high = jnp.maximum(high[a], jnp.max(s, axis=1))
        new_total = total[a] * jnp.exp(high[a] - new_high) + jnp.sum(
            jnp.exp(s - new_high[:, None]), axis=1
        )
        return high.at[a].set(new_high), total.at[a].set(new_total)

    start = (jnp.full((per_dev, pts), floor_value), jnp.zeros((per_dev, pts)))
    high, total = lax.fori_loop(0, per_dev * per_row, row_turn, start)
    src_mine = blur_scale * (mass - (high + jnp.log(total)))

    def col_turn(t, running):
        high, total = running
        a, b = t // per_row, chosen[t // per_row, t % per_row]
        s = (src_mine[a][:, None] - scores_of(a, b)) / blur_scale
        new_high = jnp.maximum(high[b], jnp.max(s, axis=0))
        new_total = total[b] * jnp.exp(high[b] - new_high) + jnp.sum(
            jnp.exp(s - new_high[None, :]), axis=0
        )
        return high.at[b].set(new_high), total.at[b].set(new_total)

    start = (jnp.full((cc, pts), floor_value), jnp.zeros((cc, pts)))
    high, total = lax.fori_loop(0, per_dev * per_row, col_turn, start)
    top = lax.pmax(high, ("row", "col"))
    total = lax.psum(total * jnp.exp(high - top), ("row", "col"))
    last = lax.dynamic_slice_in_dim(top + jnp.log(total), lax.axis_index("col") * count, count, 0)
    return lax.all_gather(src_mine, "col", axis=0, tiled=True), blur_scale * (log_dst_mass - last)


def remote(src, dst, send, recv, row, col):
    return pltpu.make_async_remote_copy(
        src_ref=src,
        dst_ref=dst,
        send_sem=send,
        recv_sem=recv,
        device_id=(row, col),
        device_id_type=pl.DeviceIdType.MESH,
    )


def greet(n_row, n_col, row, col):
    barrier = pltpu.get_barrier_semaphore()
    for j in range(1, n_row):
        pl.semaphore_signal(
            barrier,
            inc=1,
            device_id=(lax.rem(row + j, n_row), col),
            device_id_type=pl.DeviceIdType.MESH,
        )
    for j in range(1, n_col):
        pl.semaphore_signal(
            barrier,
            inc=1,
            device_id=(row, lax.rem(col + j, n_col)),
            device_id_type=pl.DeviceIdType.MESH,
        )
    pl.semaphore_wait(barrier, n_row + n_col - 2)


def spread_kernel(
    src_ref, dst_ref, pot_ref, x_ref, y_ref, g_ref, own, x_send, x_recv, g_send, g_recv,
    row_send, y_send, pair_send, y_recv,
):
    n_col, n_row = y_ref.shape[:2]
    per_dev = x_ref.shape[1]
    n_y = n_col // 2
    row, col = lax.axis_index("row"), lax.axis_index("col")
    pair = col + 1 - 2 * lax.rem(col, 2)
    kept = (
        pltpu.make_async_copy(dst_ref, y_ref.at[col, row], own.at[0]),
        pltpu.make_async_copy(
            src_ref.at[pl.ds(col * per_dev, per_dev)], x_ref.at[col], own.at[1]
        ),
        pltpu.make_async_copy(pot_ref, g_ref.at[col], own.at[2]),
    )
    for copy in kept:
        copy.start()
    greet(n_row, n_col, row, col)

    def to_row(j):
        there = lax.rem(row + j, n_row)
        return remote(
            dst_ref, y_ref.at[col, row], row_send.at[j], y_recv.at[col, row], there, col
        )

    def to_y(i, dy):
        at = lax.rem(row + n_row - i, n_row)
        block = y_ref.at[col, at]
        there = lax.rem(col + 2 * dy, n_col)
        return remote(block, block, y_send.at[dy, i], y_recv.at[col, at], row, there)

    def to_pair(i, dy):
        at = lax.rem(row + n_row - i, n_row)
        origin = lax.rem(col + n_col - 2 * dy, n_col)
        block = y_ref.at[origin, at]
        return remote(block, block, pair_send.at[dy, i], y_recv.at[origin, at], row, pair)

    def arrived(origin, at):
        block = y_ref.at[origin, at]
        remote(block, block, row_send.at[0], y_recv.at[origin, at], row, pair).wait_recv()

    def to_col(j):
        there = lax.rem(col + j, n_col)
        return (
            remote(
                src_ref.at[pl.ds(there * per_dev, per_dev)],
                x_ref.at[col], x_send.at[j], x_recv.at[col], row, there,
            ),
            remote(pot_ref, g_ref.at[col], g_send.at[j], g_recv.at[col], row, there),
        )

    for j in range(1, n_row):
        to_row(j).start()
    kept[0].wait()
    for dy in range(1, n_y):
        to_y(0, dy).start()
    to_pair(0, 0).start()
    for j in range(1, n_col):
        for copy in to_col(j):
            copy.start()

    def hand_on(i):
        at = lax.rem(row + n_row - i, n_row)
        for dy in range(1, n_y):
            arrived(lax.rem(col + n_col - 2 * dy, n_col), at)
            to_pair(i, dy).start()

    def step(i, carry):
        arrived(col, lax.rem(row + n_row - i, n_row))
        for dy in range(1, n_y):
            to_y(i, dy).start()
        to_pair(i, 0).start()
        hand_on(i - 1)
        return carry

    lax.fori_loop(1, n_row, step, 0)
    hand_on(n_row - 1)

    def finish(i, carry):
        for dy in range(n_y):
            arrived(lax.rem(pair + 2 * dy, n_col), i)
            to_pair(i, dy).wait_send()
            if dy > 0:
                to_y(i, dy).wait_send()
        return carry

    lax.fori_loop(0, n_row, finish, 0)
    for j in range(1, n_row):
        to_row(j).wait_send()
    for j in range(1, n_col):
        for copy in to_col(j):
            copy.wait_send()
        origin = lax.rem(col + j, n_col)
        remote(
            x_ref.at[origin], x_ref.at[origin], x_send.at[j], x_recv.at[origin], row, pair
        ).wait_recv()
        remote(
            g_ref.at[origin], g_ref.at[origin], g_send.at[j], g_recv.at[origin], row, pair
        ).wait_recv()
    kept[1].wait()
    kept[2].wait()


def spread(n_row, n_col, src_points, dst_points, dst_potential):
    sources, dims, pts = src_points.shape
    per_dev = sources // n_col
    sem = pltpu.SemaphoreType.DMA
    anywhere = pl.BlockSpec(memory_space=pl.ANY)
    return pl.pallas_call(
        spread_kernel,
        out_shape=(
            jax.ShapeDtypeStruct((n_col, per_dev, dims, pts), src_points.dtype),
            jax.ShapeDtypeStruct((n_col, n_row) + dst_points.shape, dst_points.dtype),
            jax.ShapeDtypeStruct((n_col,) + dst_potential.shape, jnp.float32),
        ),
        in_specs=[anywhere] * 3,
        out_specs=(anywhere,) * 3,
        scratch_shapes=[
            sem((3,)),
            sem((n_col,)),
            sem((n_col,)),
            sem((n_col,)),
            sem((n_col,)),
            sem((n_row,)),
            sem((n_col // 2, n_row)),
            sem((n_col // 2, n_row)),
            sem((n_col, n_row)),
        ],
        compiler_params=pltpu.CompilerParams(collective_id=0, has_side_effects=True),
        name="spread",
    )(src_points, dst_points, dst_potential)


def merge_kernel(
    part_ref, src_ref, mass_ref, pot_ref, new_src, new_dst, bad_ref, by_col, by_row, srcs, bads,
    part_send, part_recv, src_send, src_recv, row_send, row_recv, bad_send, bad_recv,
):
    n_col = by_col.shape[0]
    n_row = by_row.shape[0]
    per_dev = src_ref.shape[0]
    row, col = lax.axis_index("row"), lax.axis_index("col")
    greet(n_row, n_col, row, col)
    started = []
    for j in range(1, n_col):
        there = lax.rem(col + j, n_col)
        started.append(
            remote(
                part_ref.at[there], by_col.at[col], part_send.at[j], part_recv.at[col], row, there
            )
        )
        started[-1].start()
    for j in range(1, n_col):
        there = lax.rem(col + j, n_col)
        started.append(
            remote(src_ref, srcs.at[col], src_send.at[j], src_recv.at[col], row, there)
        )
        started[-1].start()
    by_col[col] = part_ref[col]
    srcs[col] = src_ref[...]

    def arrivals(held, sems, me, count):
        for j in range(1, count):
            at = lax.rem(me + j, count)
            near = lax.rem(col + 1, n_col)
            remote(held.at[at], held.at[at], bad_send.at[0], sems.at[at], row, near).wait_recv()

    arrivals(by_col, part_recv, col, n_col)
    total = by_col[0]
    for c in range(1, n_col):
        total = total + by_col[c]
    by_row[row] = total
    for j in range(1, n_row):
        there = lax.rem(row + j, n_row)
        block = by_row.at[row]
        started.append(remote(block, block, row_send.at[j], row_recv.at[row], there, col))
        started[-1].start()
    arrivals(srcs, src_recv, col, n_col)
    for c in range(n_col):
        new_src[c * per_dev : (c + 1) * per_dev, :] = srcs[c]
    arrivals(by_row, row_recv, row, n_row)
    total = by_row[0]
    for r in range(1, n_row):
        total = total + by_row[r]
    bad = jnp.where((total >= col_low) & (total <= col_top), 0.0, 1.0)
    bad = jnp.max(jnp.max(bad, axis=1, keepdims=True), axis=0, keepdims=True)
    bads[col] = jnp.broadcast_to(bad, bads.shape[1:])
    for j in range(1, n_col):
        there = lax.rem(col + j, n_col)
        block = bads.at[col]
        started.append(remote(block, block, bad_send.at[j], bad_recv.at[col], row, there))
        started[-1].start()
    new_dst[...] = blur_scale * (mass_ref[...] - (jnp.log(total) - 2.0 * pot_ref[...]))
    arrivals(bads, bad_recv, col, n_col)
    worst = bads[0]
    for c in range(1, n_col):
        worst = jnp.maximum(worst, bads[c])
    bad_ref[...] = worst
    for copy in started:
        copy.wait_send()


def merge(n_row, part, src_mine, log_dst_mass, dst_potential):
    n_col, count, pts = part.shape
    per_dev = src_mine.shape[0]
    sem = pltpu.SemaphoreType.DMA
    vmem = pl.BlockSpec(memory_space=pltpu.VMEM)
    return pl.pallas_call(
        merge_kernel,
        out_shape=(
            jax.ShapeDtypeStruct((n_col * per_dev, pts), jnp.float32),
            jax.ShapeDtypeStruct((count, pts), jnp.float32),
            jax.ShapeDtypeStruct((8, 128), jnp.float32),
        ),
        in_specs=[vmem] * 4,
        out_specs=(vmem,) * 3,
        scratch_shapes=[
            pltpu.VMEM((n_col, count, pts), jnp.float32),
            pltpu.VMEM((n_row, count, pts), jnp.float32),
            pltpu.VMEM((n_col, per_dev, pts), jnp.float32),
            pltpu.VMEM((n_col, 8, 128), jnp.float32),
            sem((n_col,)),
            sem((n_col,)),
            sem((n_col,)),
            sem((n_col,)),
            sem((n_row,)),
            sem((n_row,)),
            sem((n_col,)),
            sem((n_col,)),
        ],
        compiler_params=pltpu.CompilerParams(collective_id=1, has_side_effects=True),
        name="merge",
    )(part, src_mine, log_dst_mass, dst_potential)


def body(n_row, n_col, src_points, dst_points, support, log_src_mass, log_dst_mass, dst_potential):
    per_dev = support.shape[0] // n_col
    x_mine, y_all, g_all = spread(n_row, n_col, src_points, dst_points, dst_potential)
    src_mine, part = tiles(per_dev, support, x_mine, y_all, g_all, log_src_mass)
    src_new, dst_new, bad = merge(n_row, part, src_mine, log_dst_mass, dst_potential)
    return lax.cond(
        bad[0, 0] < 0.5,
        lambda: (src_new, dst_new),
        lambda: exact_path(
            per_dev, support, x_mine, y_all, g_all, log_src_mass, log_dst_mass
        ),
    )


def solution(mesh):
    return jax.shard_map(
        functools.partial(body, mesh.shape["row"], mesh.shape["col"]),
        mesh=mesh,
        in_specs=(
            P("row", "col", None),
            P("col", "row", None),
            P("row", None),
            P("row", None),
            P("col", None),
            P("col", None),
        ),
        out_specs=(P("row", None), P("col", None)),
        check_vma=False,
    )
```
